512 devices in a mesh: blk: 128 (over z, y, core), feat: 4 (over x).
Axes of the slice: x: 4, y: 8, z: 8, core: 2. Of those that a mesh axis runs over, the one named last changes fastest.
Arguments:
- feat_a: bfloat16 [2048, 64, 256], P('blk', 'feat'), may hold values from -25 to 25
- tiles_a: bfloat16 [2048, 8, 64, 64], P('blk', None, None, 'feat'), may hold values from -0.25 to 0.25
- owner_a: int32 [2048, 8], replicated, may hold values from 0 to 127, all different within a row; in each aligned block of 16 rows (0 to 15, 16 to 31, ...) at most 2 rows name the same one
- local_a: int32 [2048, 8], replicated, may hold values from 0 to 15
- feat_b: bfloat16 [2048, 64, 256], P('blk', 'feat'), may hold values from -25 to 25
- tiles_b: bfloat16 [2048, 8, 64, 64], P('blk', None, None, 'feat'), may hold values from -0.25 to 0.25
- owner_b: int32 [2048, 8], replicated, may hold values from 0 to 127, all different within a row; in each aligned block of 16 rows (0 to 15, 16 to 31, ...) at most 2 rows name the same one
- local_b: int32 [2048, 8], replicated, may hold values from 0 to 15
- weight: bfloat16 [256, 256], replicated, may hold values from -0.375 to 0.375
- cand_owner: int32 [256, 96], replicated, may hold values from 0 to 127, all different within a row; in each aligned block of 2 rows (0 to 1, 2 to 3, ...) at most 2 rows name the same one
- cand_local: int32 [256, 96], replicated, may hold values from 0 to 15
- target: int32 [2048, 64], P('blk'), may hold values from 0 to 6143
Outputs:
- grad_a: float32 [2048, 64, 256], P('blk', 'feat')
- grad_b: float32 [2048, 64, 256], P('blk', 'feat')
The draws below stay inside these ranges and needn't reach their ends.
Inputs may be any that keep to these rules, and one draw needn't show every extreme that they name: `owner_a`: each row names 8 different blk indices; among the 16 rows of one blk index no value is named by more than 2 rows, and in every draw some value is named by exactly 2 rows of some blk index. `owner_b`: each row names 8 different blk indices; among the 16 rows of one blk index no value is named by more than 2 rows, and in every draw some value is named by exactly 2 rows of some blk index. `cand_owner`: each row names 96 different blk indices; in the aligned blocks of 2 rows (the groups of one blk index) no value is named by more than 2 rows, and in every draw some value is named by exactly 2 rows of some block.
All inputs are finite; a program needn't handle non-finite values.
Results may differ from the reference program's by a relative error of at most 0.029.
The reference program's roundings to bfloat16 on the way count: a program that leaves them out, or rounds other values in their place, can miss the bound.
Values may be sent and summed in bfloat16 or wider, within the bound.
No kernel may reach another device: no remote copies, remote signals or barrier semaphores. Data moves between devices by JAX's collectives and lax.ppermute only.
A program may use at most 64 MiB of HBM per device.

```python
import math
import jax
import jax.numpy as jnp
import numpy as np
from jax import lax

D = 256
TB = 64
K = 8
GA = 8
BPD = 16
NB = 2048
NG = 256
CP = 96
MOST_G = 2
MOST_S = 2
N_BLK = 128


def drawn_rows(key):
    values = jax.random.normal(key, (NB, TB, D), jnp.float32)
    return jnp.clip(values, -6.0, 6.0).astype(jnp.bfloat16)


def draw_feat_a(key, part):
    key = jax.random.fold_in(key, 11)
    return drawn_rows(key)


def draw_feat_b(key, part):
    key = jax.random.fold_in(key, 23)
    return drawn_rows(key)


def place_ends(result, stream_key, low, high):
    spot = [jax.random.randint(jax.random.fold_in(stream_key, axis), (), 0, length) for axis, length in enumerate(result.shape)]
    widest = result.shape.index(max(result.shape))
    next_to = spot[:widest] + [(spot[widest] + 1) % result.shape[widest]] + spot[widest + 1:]
    return result.at[tuple(spot)].set(low).at[tuple(next_to)].set(high)


def levels(rng, extent, pieces, smallest, high):
    def one(position, parts):
        draws = jax.random.uniform(jax.random.fold_in(jax.random.fold_in(rng, 6), position), (parts,), jnp.float32, smallest / len(pieces), high / len(pieces))
        return jnp.repeat(jnp.exp(draws), extent[position] // parts).reshape((-1,) + (1,) * (len(extent) - position - 1))

    loudness = one(*pieces[0])
    for cut in pieces[1:]:
        loudness = loudness * one(*cut)
    return loudness


def routed_block(key, own, number, rows, count, top, bound, skew):
    order = jax.random.permutation(key, count)
    crowded, common = portions_of(count, rows * top, bound, skew, True), portions_of(count, rows * top, bound, skew, False)
    places = jnp.arange(count)

    def named(tallies, turn):
        used = int((tallies > 0).sum())
        fixed = max(1, used // 4)
        moved = fixed + (places - fixed + turn * (used - fixed)) % max(1, count - fixed)
        return jnp.zeros((count,), jnp.int32).at[order[jnp.where(places < fixed, places, moved)]].set(jnp.asarray(tallies, jnp.int32))

    tallies = jnp.where(number % 4 == 0, named(crowded, number // 4), named(common, number - number // 4 - 1))
    mixed = jax.random.permutation(jax.random.fold_in(own, 3), count)
    donor, sink = mixed[0:count // 2 * 2:2], mixed[1:count // 2 * 2:2]
    slack = jnp.minimum(tallies[donor] - 1, bound - tallies[sink]) // 2
    slack = jnp.where((donor == order[0]) | (sink == order[0]) | (tallies[sink] == 0), 0, jnp.maximum(slack, 0))
    moved = jax.random.randint(jax.random.fold_in(own, 4), (count // 2,), 0, 1 << 20) % (slack + 1)
    tallies = tallies.at[donor].add(-moved).at[sink].add(moved)
    items = jnp.searchsorted(jnp.cumsum(tallies), jnp.arange(rows * top), side="right").astype(jnp.int32)
    grid = items.reshape(top, rows).T
    grid = grid[jax.random.permutation(jax.random.fold_in(own, 1), rows)]
    turn = jax.random.randint(jax.random.fold_in(own, 2), (rows, 1), 0, top)
    return jnp.take_along_axis(grid, (jnp.arange(top)[None, :] + turn) % top, axis=1)


def portions_of(count, total, reach, lean, full):
    loads = [(1 << 20) // math.isqrt(grade ** lean) + 1 for grade in range(1, count + 1)]
    largest = reach if full else min(reach, max(-(-total // count), total * loads[0] // sum(loads)))
    least = 1 if total - largest >= count - 1 else 0
    counts, spare = [largest] + [least] * (count - 1), total - largest - least * (count - 1)
    while spare > 0:
        free = [i for i in range(1, count) if counts[i] < largest] or [i for i in range(1, count) if counts[i] < reach]
        whole, remaining = sum([loads[i] for i in free]), spare
        for i in free:
            more = min(reach - counts[i], max(1, remaining * loads[i] // whole), spare)
            counts[i] = counts[i] + more
            spare = spare - more
    return np.array(counts)


def scatter_about(own_key, dims, scale, most, cuts=(), kind=jnp.bfloat16):
    values = jax.random.normal(own_key, dims, jnp.float32) * scale
    if len(cuts) > 0:
        values = levels(own_key, dims, cuts, -0.22, 0.18) * values
    return jnp.clip(values, min=-most, max=most).astype(kind)


def setup_inputs(seed: int = 0) -> dict:
    streams_of = jax.random.split(jax.random.key(seed), 13)
    feat_a = draw_feat_a(jax.random.fold_in(streams_of[12], 71), 0)
    tiles_a = scatter_about(streams_of[1], (NB, K, TB, TB), (K * TB) ** -0.5, 0.25, ((0, 128), (3, 4)))
    owner_a_keys = jax.random.split(jax.random.fold_in(streams_of[2], 1), NB // BPD)
    owner_a_turns = jax.random.permutation(jax.random.fold_in(streams_of[2], 3), NB // BPD)
    owner_a = jax.vmap(lambda own, number: routed_block(jax.random.fold_in(streams_of[2], 2), own, number, BPD, N_BLK, K, MOST_G, 2))(owner_a_keys, owner_a_turns).reshape((NB, K))
    local_a = place_ends(jax.random.randint(streams_of[3], (NB, K), 0, BPD), jax.random.fold_in(streams_of[3], 1), 0, BPD - 1).astype(jnp.int32)
    feat_b = draw_feat_b(jax.random.fold_in(streams_of[12], 71), 0)
    tiles_b = scatter_about(streams_of[5], (NB, K, TB, TB), (K * TB) ** -0.5, 0.25, ((0, 128), (3, 4)))
    owner_b_keys = jax.random.split(jax.random.fold_in(streams_of[6], 1), NB // BPD)
    owner_b_turns = jax.random.permutation(jax.random.fold_in(streams_of[6], 3), NB // BPD)
    owner_b = jax.vmap(lambda own, number: routed_block(jax.random.fold_in(streams_of[6], 2), own, number, BPD, N_BLK, K, MOST_G, 2))(owner_b_keys, owner_b_turns).reshape((NB, K))
    local_b = place_ends(jax.random.randint(streams_of[7], (NB, K), 0, BPD), jax.random.fold_in(streams_of[7], 1), 0, BPD - 1).astype(jnp.int32)
    weight = scatter_about(streams_of[8], (D, D), D ** -0.5, 0.375)
    cand_owner_keys = jax.random.split(jax.random.fold_in(streams_of[9], 1), NG // (BPD // GA))
    cand_owner_turns = jax.random.permutation(jax.random.fold_in(streams_of[9], 3), NG // (BPD // GA))
    cand_owner = jax.vmap(lambda own, number: routed_block(jax.random.fold_in(streams_of[9], 2), own, number, BPD // GA, N_BLK, CP, MOST_S, 2))(cand_owner_keys, cand_owner_turns).reshape((NG, CP))
    cand_local = place_ends(jax.random.randint(streams_of[10], (NG, CP), 0, BPD), jax.random.fold_in(streams_of[10], 1), 0, BPD - 1).astype(jnp.int32)
    target = place_ends(jax.random.randint(streams_of[11], (NB, TB), 0, CP * TB), jax.random.fold_in(streams_of[11], 1), 0, (CP * TB) - 1).astype(jnp.int32)
    return {"feat_a": feat_a, "tiles_a": tiles_a, "owner_a": owner_a, "local_a": local_a, "feat_b": feat_b, "tiles_b": tiles_b, "owner_b": owner_b, "local_b": local_b, "weight": weight, "cand_owner": cand_owner, "cand_local": cand_local, "target": target}


score_scale = 0.25


def propagate(features, tile_set, owners, within, weight):
    columns = (owners * BPD + within).astype(jnp.int32)

    def one_block(tile_pair):
        block_tiles, chosen = tile_pair
        neighbours = jnp.take(features, chosen, axis=0).astype(jnp.float32)
        return jnp.einsum("kij,kjd->id", block_tiles.astype(jnp.float32), neighbours)

    gathered = lax.map(one_block, (tile_set, columns))
    propagated = (features.astype(jnp.float32) + gathered).astype(jnp.bfloat16).reshape(NB * TB, D)
    preact = jnp.dot(propagated, weight, preferred_element_type=jnp.float32)
    embedded = jnp.maximum(preact, 0.0).astype(jnp.bfloat16).reshape(NB, TB, D)
    return embedded


def reference(feat_a, tiles_a, owner_a, local_a, feat_b, tiles_b, owner_b, local_b, weight, cand_owner, cand_local, target):
    emb_a = propagate(feat_a, tiles_a, owner_a, local_a, weight)
    emb_b = propagate(feat_b, tiles_b, owner_b, local_b, weight)
    cand = (cand_owner * BPD + cand_local).astype(jnp.int32)
    group_rows = GA * TB
    group_queries = emb_a.reshape(NG, group_rows, D)
    group_target = target.reshape(NG, group_rows)
    column_ids = jnp.arange(CP * TB, dtype=jnp.int32)

    def one_group(accumulated, inputs):
        queries, chosen, wanted = inputs
        key_rows = jnp.take(emb_b, chosen, axis=0).reshape(CP * TB, D)
        scores = score_scale * jnp.dot(queries, key_rows.T, preferred_element_type=jnp.float32)
        highest = jnp.max(scores, axis=1, keepdims=True)
        exponent = jnp.exp(scores - highest)
        denominator = jnp.sum(exponent, axis=1, keepdims=True)
        picked = (column_ids[None, :] == wanted[:, None]).astype(jnp.float32)
        dscore = (exponent / denominator - picked).astype(jnp.bfloat16)
        query_grad = score_scale * jnp.dot(dscore, key_rows, preferred_element_type=jnp.float32)
        key_grad = score_scale * jnp.dot(dscore.T, queries, preferred_element_type=jnp.float32)
        key_term = lax.optimization_barrier(key_grad.astype(jnp.bfloat16)).astype(jnp.float32)
        accumulated = accumulated.at[chosen].add(key_term.reshape(CP, TB, D))
        return accumulated, query_grad

    grad_b, query_grads = lax.scan(one_group, jnp.zeros((NB, TB, D), jnp.float32), (group_queries, cand, group_target))
    grad_a = query_grads.reshape(NB, TB, D)
    return grad_a, grad_b
```

```python
import functools

import jax
import jax.numpy as jnp
from jax import lax
from jax.experimental import pallas as pl
from jax.experimental.pallas import tpu as pltpu
from jax.sharding import PartitionSpec as P

GA = 8
SPLITS = 4

score_scale = 0.25
hidden = -1e30


def link_sending(owner, within, peer_count, source):
    rows = owner.shape[0] // peer_count
    place = jnp.arange(rows * owner.shape[1], dtype=jnp.int32).reshape(1, rows, owner.shape[1])
    code = place * 16 + within.reshape(peer_count, rows, -1)
    present = owner.reshape(peer_count, rows, -1) == source
    first = jnp.min(jnp.where(present, code, 1 << 20), axis=(1, 2))
    last = jnp.max(jnp.where(present, code, 0), axis=(1, 2))
    return jnp.stack([first, last], axis=1).reshape(-1) & 15


def link_slots(owner, peer_count, source):
    own = lax.dynamic_index_in_dim(owner.reshape(peer_count, -1), source, 0, keepdims=False)
    count = own.shape[0]
    same = own[:, None] == own[None, :]
    before = jnp.arange(count)[None, :] < jnp.arange(count)[:, None]
    return own * 2 + jnp.any(same & before, axis=1).astype(jnp.int32)


def pick(rows, index):
    return jnp.take(rows, index, axis=0, mode="clip")


def exchange(rows, peer_count):
    blocks = rows.reshape(peer_count, 2, *rows.shape[1:])
    return lax.all_to_all(blocks, "blk", split_axis=0, concat_axis=0, tiled=True)


def aggregate(tile_set, arrived, slots):
    neighbours = pick(arrived.reshape(-1, *arrived.shape[2:]), slots)
    neighbours = neighbours.reshape(*tile_set.shape[:2], *arrived.shape[2:])
    return jnp.einsum("bkrc,bkcd->brd", tile_set, neighbours, preferred_element_type=jnp.float32)


def embedding(local_features, summed, weight):
    blocks, quarter, features = local_features.shape
    propagated = (
        (local_features.astype(jnp.float32) + summed)
        .astype(jnp.bfloat16)
        .reshape(blocks * quarter, features)
    )
    preact = jnp.dot(propagated, weight, preferred_element_type=jnp.float32)
    return jnp.maximum(preact, 0.0).astype(jnp.bfloat16).reshape(blocks, quarter, features)


def key_chunk(key_ref, step):
    owners = key_ref.shape[0] // SPLITS
    blocks = key_ref[pl.ds(step * owners, owners), 0]
    return blocks.reshape(owners * blocks.shape[1], blocks.shape[2])


def chunk_scores(keys, queries, bias):
    product = lax.dot_general(
        keys, queries, (((1,), (1,)), ((), ())), preferred_element_type=jnp.float32
    )
    return score_scale * product + bias


def stats_kernel(key_ref, query_ref, bias_ref, out_ref, score_ref):
    queries = query_ref[0]
    rows = score_ref.shape[0] // SPLITS
    top = None
    for step in range(SPLITS):
        part = pl.ds(step * rows, rows)
        scores = chunk_scores(key_chunk(key_ref, step), queries, bias_ref[0, part, :])
        score_ref[part, :] = scores
        highest = jnp.max(scores, axis=0, keepdims=True)
        top = highest if top is None else jnp.maximum(top, highest)
    total = jnp.zeros_like(top)
    for step in range(SPLITS):
        part = pl.ds(step * rows, rows)
        total = total + jnp.sum(jnp.exp(score_ref[part, :] - top), axis=0, keepdims=True)
    out_ref[0, 0:1, :] = top
    out_ref[0, 1:2, :] = total


def grads_kernel(key_ref, query_ref, bias_ref, stats_ref, wanted_ref, key_out, query_out):
    queries = query_ref[0]
    owners = key_ref.shape[0] // SPLITS
    rows = owners * key_ref.shape[2]
    tops = [stats_ref[part, 0, 0:1, :] for part in range(stats_ref.shape[0])]
    totals = [stats_ref[part, 0, 1:2, :] for part in range(stats_ref.shape[0])]
    top = functools.reduce(jnp.maximum, tops)
    denom = sum(total * jnp.exp(high - top) for high, total in zip(tops, totals))
    inverse = 1.0 / denom
    wanted = wanted_ref[0]
    gathered = None
    for step in range(SPLITS):
        keys = key_chunk(key_ref, step)
        scores = chunk_scores(keys, queries, bias_ref[0, pl.ds(step * rows, rows), :])
        probability = jnp.exp(scores - top) * inverse
        ids = lax.broadcasted_iota(jnp.int32, probability.shape, 0) + step * rows
        dscore = jnp.where(ids == wanted, probability - 1.0, probability).astype(jnp.bfloat16)
        key_term = score_scale * jnp.dot(dscore, queries, preferred_element_type=jnp.float32)
        key_out[pl.ds(step * owners, owners), 0] = key_term.astype(jnp.bfloat16).reshape(
            owners, key_ref.shape[2], key_ref.shape[3]
        )
        piece = lax.dot_general(
            dscore, keys, (((0,), (0,)), ((), ())), preferred_element_type=jnp.float32
        )
        gathered = piece if gathered is None else gathered + piece
    query_out[0] = score_scale * gathered


def score_specs(keys, queries):
    peers, groups, quarter, features = keys.shape
    rows = queries.shape[1]
    return (
        pl.BlockSpec((peers, 1, quarter, features), lambda g: (0, g, 0, 0)),
        pl.BlockSpec((1, rows, features), lambda g: (g, 0, 0)),
        pl.BlockSpec((1, peers * quarter, 1), lambda g: (g, 0, 0)),
    )


def score_stats(keys, queries, bias):
    peers, groups, quarter, features = keys.shape
    rows = queries.shape[1]
    return pl.pallas_call(
        stats_kernel,
        grid=(groups,),
        in_specs=score_specs(keys, queries),
        out_specs=pl.BlockSpec((1, 2, rows), lambda g: (g, 0, 0)),
        out_shape=jax.ShapeDtypeStruct((groups, 2, rows), jnp.float32),
        scratch_shapes=[pltpu.VMEM((peers * quarter, rows), jnp.float32)],
        compiler_params=pltpu.CompilerParams(vmem_limit_bytes=32 << 20),
        name="score_stats",
    )(keys, queries, bias)


def score_grads(keys, queries, bias, stats, wanted):
    peers, groups, quarter, features = keys.shape
    rows = queries.shape[1]
    key_spec, query_spec, bias_spec = score_specs(keys, queries)
    return pl.pallas_call(
        grads_kernel,
        grid=(groups,),
        in_specs=(
            key_spec,
            query_spec,
            bias_spec,
            pl.BlockSpec((stats.shape[0], 1, 2, rows), lambda g: (0, g, 0, 0)),
            pl.BlockSpec((1, 1, rows), lambda g: (g, 0, 0)),
        ),
        out_specs=(key_spec, query_spec),
        out_shape=(
            jax.ShapeDtypeStruct(keys.shape, jnp.bfloat16),
            jax.ShapeDtypeStruct(queries.shape, jnp.float32),
        ),
        compiler_params=pltpu.CompilerParams(vmem_limit_bytes=32 << 20),
        name="score_grads",
    )(keys, queries, bias, stats, wanted)


def per_device(
    feat_a,
    tiles_a,
    owner_a,
    local_a,
    feat_b,
    tiles_b,
    owner_b,
    local_b,
    weight,
    cand_owner,
    cand_local,
    target,
):
    peer_count = lax.axis_size("blk")
    source = lax.axis_index("blk")
    part_index = lax.axis_index("feat")
    blocks_here, quarter, features = feat_a.shape
    tile_rows = tiles_a.shape[2]
    groups_here = blocks_here // GA
    group_rows = GA * tile_rows

    arrived_b = exchange(pick(feat_b, link_sending(owner_b, local_b, peer_count, source)), peer_count)
    arrived_a = exchange(pick(feat_a, link_sending(owner_a, local_a, peer_count, source)), peer_count)
    partial_b = aggregate(tiles_b, arrived_b, link_slots(owner_b, peer_count, source))
    partial_a = aggregate(tiles_a, arrived_a, link_slots(owner_a, peer_count, source))
    summed_b = lax.psum_scatter(partial_b, "feat", scatter_dimension=1, tiled=True)
    summed_a = lax.psum_scatter(partial_a, "feat", scatter_dimension=1, tiled=True)
    emb_b = embedding(feat_b, summed_b, weight)
    emb_a = embedding(feat_a, summed_a, weight)
    full_a = lax.all_gather(emb_a, "feat", axis=1, tiled=True)
    queries = full_a.reshape(groups_here, group_rows, features)

    named = cand_owner == source
    chosen = jnp.sum(jnp.where(named, cand_local, 0), axis=1)
    filled = jnp.any(named, axis=1)
    keys = exchange(pick(emb_b, chosen), peer_count)

    own = lax.dynamic_slice_in_dim(cand_owner, source * groups_here, groups_here, 0)
    peers = jnp.arange(peer_count, dtype=jnp.int32)
    arrives = jnp.any(own[:, :, None] == peers[None, None, :], axis=1)
    bias = jnp.where(jnp.repeat(arrives, quarter, axis=1), 0.0, hidden).astype(jnp.float32)[:, :, None]
    wanted = target.reshape(groups_here, group_rows)
    column = wanted // tile_rows
    row = wanted % tile_rows
    listed = jnp.arange(cand_owner.shape[1], dtype=jnp.int32)
    holder = jnp.sum(
        jnp.where(column[:, :, None] == listed[None, None, :], own[:, None, :], 0), axis=2
    )
    inside = row // quarter == part_index
    wanted = jnp.where(inside, holder * quarter + row % quarter, -1)[:, None, :]

    stats = lax.all_gather(score_stats(keys, queries, bias), "feat", axis=0)
    key_terms, query_terms = score_grads(keys, queries, bias, stats, wanted)

    query_terms = query_terms.reshape(groups_here, GA, tile_rows, features)
    grad_a = lax.psum_scatter(query_terms, "feat", scatter_dimension=2, tiled=True).reshape(
        blocks_here, quarter, features
    )
    returned = lax.all_to_all(key_terms, "blk", split_axis=0, concat_axis=0, tiled=True)
    holds = (jnp.arange(blocks_here, dtype=jnp.int32)[None, :] == chosen[:, None]) & filled[:, None]
    grad_b = jnp.einsum(
        "sb,srd->brd",
        holds.astype(jnp.bfloat16),
        returned.reshape(-1, quarter, features),
        preferred_element_type=jnp.float32,
    )
    return (grad_a, grad_b)


def solution(mesh):
    placed = (
        P("blk", "feat", None),
        P("blk", None, None, "feat"),
        P(),
        P(),
        P("blk", "feat", None),
        P("blk", None, None, "feat"),
        P(),
        P(),
        P(),
        P(),
        P(),
        P("blk", None),
    )
    return jax.shard_map(
        per_device,
        mesh=mesh,
        in_specs=placed,
        out_specs=(P("blk", "feat", None), P("blk", "feat", None)),
        check_vma=False,
    )
```

```python
import functools

import jax
import jax.numpy as jnp
from jax import lax
from jax.experimental import pallas as pl
from jax.experimental.pallas import tpu as pltpu
from jax.sharding import PartitionSpec as P

GA = 8
SPLITS = 4

score_scale = 0.25
hidden = -1e30


def link_sending(owner, within, peer_count, source):
    rows = owner.shape[0] // peer_count
    place = jnp.arange(rows * owner.shape[1], dtype=jnp.int32).reshape(1, rows, owner.shape[1])
    code = place * 16 + within.reshape(peer_count, rows, -1)
    present = owner.reshape(peer_count, rows, -1) == source
    first = jnp.min(jnp.where(present, code, 1 << 20), axis=(1, 2))
    last = jnp.max(jnp.where(present, code, 0), axis=(1, 2))
    return jnp.stack([first, last], axis=1).reshape(-1) & 15


def link_slots(owner, peer_count, source):
    own = lax.dynamic_index_in_dim(owner.reshape(peer_count, -1), source, 0, keepdims=False)
    count = own.shape[0]
    same = own[:, None] == own[None, :]
    before = jnp.arange(count)[None, :] < jnp.arange(count)[:, None]
    return own * 2 + jnp.any(same & before, axis=1).astype(jnp.int32)


def pick(rows, index):
    return jnp.take(rows, index, axis=0, mode="clip")


def exchange(rows, peer_count):
    blocks = rows.reshape(peer_count, 2, *rows.shape[1:])
    return lax.all_to_all(blocks, "blk", split_axis=0, concat_axis=0, tiled=True)


def aggregate(tile_set, arrived, slots):
    neighbours = pick(arrived.reshape(-1, *arrived.shape[2:]), slots)
    neighbours = neighbours.reshape(*tile_set.shape[:2], *arrived.shape[2:])
    return jnp.einsum("bkrc,bkcd->brd", tile_set, neighbours, preferred_element_type=jnp.float32)


def embedding(local_features, summed, weight):
    blocks, quarter, features = local_features.shape
    propagated = (
        (local_features.astype(jnp.float32) + summed)
        .astype(jnp.bfloat16)
        .reshape(blocks * quarter, features)
    )
    preact = jnp.dot(propagated, weight, preferred_element_type=jnp.float32)
    return jnp.maximum(preact, 0.0).astype(jnp.bfloat16).reshape(blocks, quarter, features)


def scatter_sum(partial, part_index, parts):
    blocks, rows, features = partial.shape
    pieces = partial.reshape(blocks, parts, rows // parts, features)
    total = lax.dynamic_index_in_dim(pieces, part_index, 1, keepdims=False)
    for shift in range(1, parts):
        piece = lax.dynamic_index_in_dim(pieces, (part_index + shift) % parts, 1, keepdims=False)
        moves = [(i, (i + shift) % parts) for i in range(parts)]
        total = total + lax.ppermute(piece, "feat", moves)
    return total


def gather_rows(quarter_rows, part_index, parts):
    blocks, quarter, features = quarter_rows.shape
    held = [quarter_rows]
    for shift in range(1, parts):
        moves = [(i, (i + shift) % parts) for i in range(parts)]
        held.append(lax.ppermute(quarter_rows, "feat", moves))
    back = (part_index - jnp.arange(parts, dtype=jnp.int32)) % parts
    ordered = pick(jnp.stack(held), back)
    return jnp.moveaxis(ordered, 0, 1).reshape(blocks, parts * quarter, features)


def collect_stats(stats, parts):
    held = stats[None]
    for flip in (1, 3):
        moves = [(i, i ^ flip) for i in range(parts)]
        held = jnp.concatenate([held, lax.ppermute(held, "feat", moves)], axis=0)
    return held


def key_chunk(key_ref, step):
    owners = key_ref.shape[0] // SPLITS
    blocks = key_ref[pl.ds(step * owners, owners), 0]
    return blocks.reshape(owners * blocks.shape[1], blocks.shape[2])


def chunk_scores(keys, queries, bias):
    product = lax.dot_general(
        keys, queries, (((1,), (1,)), ((), ())), preferred_element_type=jnp.float32
    )
    return score_scale * product + bias


def stats_kernel(key_ref, query_ref, bias_ref, out_ref, score_ref):
    queries = query_ref[0]
    rows = score_ref.shape[0] // SPLITS
    top = None
    for step in range(SPLITS):
        part = pl.ds(step * rows, rows)
        scores = chunk_scores(key_chunk(key_ref, step), queries, bias_ref[0, part, :])
        score_ref[part, :] = scores
        highest = jnp.max(scores, axis=0, keepdims=True)
        top = highest if top is None else jnp.maximum(top, highest)
    total = jnp.zeros_like(top)
    for step in range(SPLITS):
        part = pl.ds(step * rows, rows)
        total = total + jnp.sum(jnp.exp(score_ref[part, :] - top), axis=0, keepdims=True)
    out_ref[0, 0:1, :] = top
    out_ref[0, 1:2, :] = total


def grads_kernel(key_ref, query_ref, bias_ref, stats_ref, wanted_ref, key_out, query_out):
    queries = query_ref[0]
    owners = key_ref.shape[0] // SPLITS
    rows = owners * key_ref.shape[2]
    tops = [stats_ref[part, 0, 0:1, :] for part in range(stats_ref.shape[0])]
    totals = [stats_ref[part, 0, 1:2, :] for part in range(stats_ref.shape[0])]
    top = functools.reduce(jnp.maximum, tops)
    denom = sum(total * jnp.exp(high - top) for high, total in zip(tops, totals))
    inverse = 1.0 / denom
    wanted = wanted_ref[0]
    gathered = None
    for step in range(SPLITS):
        keys = key_chunk(key_ref, step)
        scores = chunk_scores(keys, queries, bias_ref[0, pl.ds(step * rows, rows), :])
        probability = jnp.exp(scores - top) * inverse
        ids = lax.broadcasted_iota(jnp.int32, probability.shape, 0) + step * rows
        dscore = jnp.where(ids == wanted, probability - 1.0, probability).astype(jnp.bfloat16)
        key_term = score_scale * jnp.dot(dscore, queries, preferred_element_type=jnp.float32)
        key_out[pl.ds(step * owners, owners), 0] = key_term.astype(jnp.bfloat16).reshape(
            owners, key_ref.shape[2], key_ref.shape[3]
        )
        piece = lax.dot_general(
            dscore, keys, (((0,), (0,)), ((), ())), preferred_element_type=jnp.float32
        )
        gathered = piece if gathered is None else gathered + piece
    query_out[0] = score_scale * gathered


def score_specs(keys, queries):
    peers, groups, quarter, features = keys.shape
    rows = queries.shape[1]
    return (
        pl.BlockSpec((peers, 1, quarter, features), lambda g: (0, g, 0, 0)),
        pl.BlockSpec((1, rows, features), lambda g: (g, 0, 0)),
        pl.BlockSpec((1, peers * quarter, 1), lambda g: (g, 0, 0)),
    )


def score_stats(keys, queries, bias):
    peers, groups, quarter, features = keys.shape
    rows = queries.shape[1]
    return pl.pallas_call(
        stats_kernel,
        grid=(groups,),
        in_specs=score_specs(keys, queries),
        out_specs=pl.BlockSpec((1, 2, rows), lambda g: (g, 0, 0)),
        out_shape=jax.ShapeDtypeStruct((groups, 2, rows), jnp.float32),
        scratch_shapes=[pltpu.VMEM((peers * quarter, rows), jnp.float32)],
        compiler_params=pltpu.CompilerParams(vmem_limit_bytes=32 << 20),
        name="score_stats",
    )(keys, queries, bias)


def score_grads(keys, queries, bias, stats, wanted):
    peers, groups, quarter, features = keys.shape
    rows = queries.shape[1]
    key_spec, query_spec, bias_spec = score_specs(keys, queries)
    return pl.pallas_call(
        grads_kernel,
        grid=(groups,),
        in_specs=(
            key_spec,
            query_spec,
            bias_spec,
            pl.BlockSpec((stats.shape[0], 1, 2, rows), lambda g: (0, g, 0, 0)),
            pl.BlockSpec((1, 1, rows), lambda g: (g, 0, 0)),
        ),
        out_specs=(key_spec, query_spec),
        out_shape=(
            jax.ShapeDtypeStruct(keys.shape, jnp.bfloat16),
            jax.ShapeDtypeStruct(queries.shape, jnp.float32),
        ),
        compiler_params=pltpu.CompilerParams(vmem_limit_bytes=32 << 20),
        name="score_grads",
    )(keys, queries, bias, stats, wanted)


def per_device(
    feat_a,
    tiles_a,
    owner_a,
    local_a,
    feat_b,
    tiles_b,
    owner_b,
    local_b,
    weight,
    cand_owner,
    cand_local,
    target,
):
    peer_count = lax.axis_size("blk")
    source = lax.axis_index("blk")
    part_index = lax.axis_index("feat")
    parts = lax.axis_size("feat")
    blocks_here, quarter, features = feat_a.shape
    tile_rows = tiles_a.shape[2]
    groups_here = blocks_here // GA
    group_rows = GA * tile_rows

    arrived_b = exchange(pick(feat_b, link_sending(owner_b, local_b, peer_count, source)), peer_count)
    arrived_a = exchange(pick(feat_a, link_sending(owner_a, local_a, peer_count, source)), peer_count)
    partial_b = aggregate(tiles_b, arrived_b, link_slots(owner_b, peer_count, source))
    partial_a = aggregate(tiles_a, arrived_a, link_slots(owner_a, peer_count, source))
    summed_b = scatter_sum(partial_b, part_index, parts)
    summed_a = scatter_sum(partial_a, part_index, parts)
    emb_b = embedding(feat_b, summed_b, weight)
    emb_a = embedding(feat_a, summed_a, weight)
    full_a = gather_rows(emb_a, part_index, parts)
    queries = full_a.reshape(groups_here, group_rows, features)

    named = cand_owner == source
    chosen = jnp.sum(jnp.where(named, cand_local, 0), axis=1)
    filled = jnp.any(named, axis=1)
    keys = exchange(pick(emb_b, chosen), peer_count)

    own = lax.dynamic_slice_in_dim(cand_owner, source * groups_here, groups_here, 0)
    peers = jnp.arange(peer_count, dtype=jnp.int32)
    arrives = jnp.any(own[:, :, None] == peers[None, None, :], axis=1)
    bias = jnp.where(jnp.repeat(arrives, quarter, axis=1), 0.0, hidden).astype(jnp.float32)[:, :, None]
    wanted = target.reshape(groups_here, group_rows)
    column = wanted // tile_rows
    row = wanted % tile_rows
    listed = jnp.arange(cand_owner.shape[1], dtype=jnp.int32)
    holder = jnp.sum(
        jnp.where(column[:, :, None] == listed[None, None, :], own[:, None, :], 0), axis=2
    )
    inside = row // quarter == part_index
    wanted = jnp.where(inside, holder * quarter + row % quarter, -1)[:, None, :]

    stats = collect_stats(score_stats(keys, queries, bias), parts)
    key_terms, query_terms = score_grads(keys, queries, bias, stats, wanted)

    query_terms = query_terms.reshape(blocks_here, tile_rows, features)
    grad_a = scatter_sum(query_terms, part_index, parts)
    returned = lax.all_to_all(key_terms, "blk", split_axis=0, concat_axis=0, tiled=True)
    holds = (jnp.arange(blocks_here, dtype=jnp.int32)[None, :] == chosen[:, None]) & filled[:, None]
    grad_b = jnp.einsum(
        "sb,srd->brd",
        holds.astype(jnp.bfloat16),
        returned.reshape(-1, quarter, features),
        preferred_element_type=jnp.float32,
    )
    return (grad_a, grad_b)


def solution(mesh):
    placed = (
        P("blk", "feat", None),
        P("blk", None, None, "feat"),
        P(),
        P(),
        P("blk", "feat", None),
        P("blk", None, None, "feat"),
        P(),
        P(),
        P(),
        P(),
        P(),
        P("blk", None),
    )
    return jax.shard_map(
        per_device,
        mesh=mesh,
        in_specs=placed,
        out_specs=(P("blk", "feat", None), P("blk", "feat", None)),
        check_vma=False,
    )
```
